32 devices in a mesh: node: 16 (over z, y, x), state: 2 (over core).
Axes of the slice: x: 2, y: 2, z: 4, core: 2. Of those that a mesh axis runs over, the one named last changes fastest.
Arguments:
- wavefunctions: float32 [16384, 8192], P('node', 'state'), may hold values from -0.53033006 to 0.53033006
- h_wavefunctions: float32 [16384, 8192], P('node', 'state'), may hold values from -0.53033006 to 0.53033006
- block_ids: int32 [4], replicated, may hold values from 0 to 63, as said below
Outputs:
- correlation: float32 [8192, 512], P(('state', 'node'))
- projected: float32 [8192, 512], P(('state', 'node'))
The draws below stay inside these ranges and needn't reach their ends.
Inputs may be any that keep to these rules, and one draw needn't show every extreme that they name: `block_ids`: the 4 block numbers are distinct, and among them are always the first and the last block.
All inputs are finite; a program needn't handle non-finite values.
Results may differ from the reference program's by a relative error of at most 0.0001.
Values sent between devices are 32-bit elements; how exact they have to be, the bound alone decides.
No kernel may reach another device: no remote copies, remote signals or barrier semaphores. Data moves between devices by JAX's collectives and lax.ppermute only.
A program may use at most 192 MiB of HBM per device.

```python
import jax
import jax.numpy as jnp
from jax import lax

STATES = 8192
BLOCK = 128
NBLK = 4
NODES = 16384


def draw_block_ids(key, part):
    key = jax.random.fold_in(key, 5)
    first_key, second_key = jax.random.split(key)
    count = STATES // BLOCK
    others = (jax.random.permutation(first_key, count - 2)[:NBLK - 2] + 1).astype(jnp.int32)
    chosen = jnp.concatenate([others, jnp.zeros((1,), jnp.int32), jnp.full((1,), count - 1, jnp.int32)])
    return jax.random.permutation(second_key, chosen).astype(jnp.int32)


def spiked(values, own_key, source, target, blocks, factor):
    def block_of(position):
        return (jnp.arange(values.shape[position]) // (values.shape[position] // blocks)).reshape((-1,) + (1,) * (values.ndim - 1 - position))

    first = jax.random.permutation(own_key, blocks)[block_of(target)]
    far = (block_of(target) + blocks // 2) % blocks
    return jnp.where((block_of(source) == first) | (block_of(source) == far), factor * values, values)


def levels(own_key, dims, shards, least, largest):
    gain = 1.0
    for axis_at, parts in shards:
        heights = jax.random.uniform(jax.random.fold_in(jax.random.fold_in(own_key, 6), axis_at), (parts,), jnp.float32, least / len(shards), largest / len(shards))
        gain = gain * jnp.repeat(jnp.exp(heights), dims[axis_at] // parts).reshape((-1,) + (1,) * (len(dims) - 1 - axis_at))
    return gain


def heavy_noise(rng, shape, width, limit, pieces, heavy, held_as=jnp.bfloat16):
    result = width * jax.random.normal(rng, shape, jnp.float32)
    if pieces:
        result = result * levels(rng, shape, pieces, -0.22, 0.18)
    return jnp.clip(spiked(result, jax.random.fold_in(rng, 3), *heavy), -limit, limit).astype(held_as)


def setup_inputs(seed: int = 0) -> dict:
    streams_of = jax.random.split(jax.random.key(seed), 4)
    wavefunctions = heavy_noise(streams_of[0], (NODES, STATES), (NODES ** -0.25), 0.53033006, ((0, 16), (1, 2)), (0, 1, 16, 2.0), jnp.float32)
    h_wavefunctions = heavy_noise(streams_of[1], (NODES, STATES), (NODES ** -0.25), 0.53033006, ((0, 16), (1, 2)), (0, 1, 16, 2.0), jnp.float32)
    block_ids = draw_block_ids(jax.random.fold_in(streams_of[3], 71), 0)
    return {"wavefunctions": wavefunctions, "h_wavefunctions": h_wavefunctions, "block_ids": block_ids}


def reference(wavefunctions, h_wavefunctions, block_ids):
    correlation_cols = []
    energy_cols = []
    for step in range(NBLK):
        start = (block_ids[step] * BLOCK).astype(jnp.int32)
        psi_block = lax.dynamic_slice_in_dim(wavefunctions, start, BLOCK, 1)
        hpsi_block = lax.dynamic_slice_in_dim(h_wavefunctions, start, BLOCK, 1)
        correlation_cols.append(jnp.dot(wavefunctions.T, psi_block, preferred_element_type=jnp.float32, precision=lax.Precision.HIGHEST))
        energy_cols.append(jnp.dot(wavefunctions.T, hpsi_block, preferred_element_type=jnp.float32, precision=lax.Precision.HIGHEST))
    return jnp.concatenate(correlation_cols, axis=1), jnp.concatenate(energy_cols, axis=1)
```

```python
import functools

import jax
import jax.numpy as jnp
from jax import lax
from jax.experimental import pallas as pl
from jax.experimental.pallas import tpu as pltpu
from jax.sharding import PartitionSpec as P

BLOCK = 128
NBLK = 4
LANES = 128

BITS = {"x": 1, "y": 2, "z": 4, "w": 8}

PARTS = (
    ("xyzw", 88), ("yxzw", 88), ("zxyw", 80),
    ("xyzw", 88), ("yxzw", 88), ("zyxw", 80),
    ("xyzw", 88), ("yxzw", 88), ("zxyw", 80),
    ("xyzw", 88), ("yxzw", 88), ("zyxw", 80),
)


def split(value):
    high = value.astype(jnp.bfloat16)
    low = (value - high.astype(jnp.float32)).astype(jnp.bfloat16)
    return high, low


def dot3(left, right):
    left_high, left_low = left
    right_high, right_low = right
    dot = functools.partial(jnp.dot, preferred_element_type=jnp.float32)
    return dot(left_high, right_high) + (dot(left_high, right_low) + dot(left_low, right_high))


def columns_kernel(places, psi_ref, hpsi_ref, out_ref):
    out_ref[0, :BLOCK, :] = psi_ref[...].T
    out_ref[0, BLOCK:, :] = hpsi_ref[...].T


def block_columns(wavefunctions, h_wavefunctions, places):
    nodes = wavefunctions.shape[0]
    count = places.shape[0]
    source = pl.BlockSpec((nodes, BLOCK), lambda i, places: (0, places[i]))
    return pl.pallas_call(
        columns_kernel,
        grid_spec=pltpu.PrefetchScalarGridSpec(
            num_scalar_prefetch=1,
            grid=(count,),
            in_specs=[source, source],
            out_specs=pl.BlockSpec((1, 2 * BLOCK, nodes), lambda i, places: (i, 0, 0)),
        ),
        out_shape=jax.ShapeDtypeStruct((count, 2 * BLOCK, nodes), jnp.float32),
        compiler_params=pltpu.CompilerParams(vmem_limit_bytes=24 << 20),
        cost_estimate=pl.CostEstimate(
            flops=0, bytes_accessed=count * 4 * BLOCK * nodes * 4, transcendentals=0
        ),
        name="block_columns",
    )(places, wavefunctions, h_wavefunctions)


def partial_kernel(groups, columns_ref, states_ref, out_ref, high_ref, low_ref):
    @pl.when(pl.program_id(0) == 0)
    def _():
        high_ref[...], low_ref[...] = split(columns_ref[...])

    out_ref[0] = dot3((high_ref[...], low_ref[...]), split(states_ref[...]))


def partial_sums(wavefunctions, columns, groups, share_rows):
    nodes = wavefunctions.shape[0]
    width = columns.shape[0]
    count = groups.shape[0]
    return pl.pallas_call(
        partial_kernel,
        grid_spec=pltpu.PrefetchScalarGridSpec(
            num_scalar_prefetch=1,
            grid=(count,),
            in_specs=[
                pl.BlockSpec((width, nodes), lambda i, groups: (0, 0)),
                pl.BlockSpec((nodes, share_rows), lambda i, groups: (0, groups[i])),
            ],
            out_specs=pl.BlockSpec((1, width, share_rows), lambda i, groups: (i, 0, 0)),
            scratch_shapes=[
                pltpu.VMEM((width, nodes), jnp.bfloat16),
                pltpu.VMEM((width, nodes), jnp.bfloat16),
            ],
        ),
        out_shape=jax.ShapeDtypeStruct((count, width, share_rows), jnp.float32),
        compiler_params=pltpu.CompilerParams(vmem_limit_bytes=24 << 20),
        cost_estimate=pl.CostEstimate(
            flops=6 * count * width * share_rows * nodes,
            bytes_accessed=4 * (count * share_rows * (nodes + width) + width * nodes),
            transcendentals=0,
        ),
        name="partial_sums",
    )(groups, columns, wavefunctions)


def place_kernel(slots, sums_ref, correlation_ref, energy_ref):
    correlation_ref[...] = sums_ref[0, :BLOCK, :].T
    energy_ref[...] = sums_ref[0, BLOCK:, :].T


def place_columns(sums, slots, share_rows):
    out = jax.ShapeDtypeStruct((share_rows, NBLK * BLOCK), jnp.float32)
    target = pl.BlockSpec((share_rows, BLOCK), lambda i, slots: (0, slots[i]))
    return pl.pallas_call(
        place_kernel,
        grid_spec=pltpu.PrefetchScalarGridSpec(
            num_scalar_prefetch=1,
            grid=(NBLK,),
            in_specs=[pl.BlockSpec((1, 2 * BLOCK, share_rows), lambda i, slots: (i, 0, 0))],
            out_specs=[target, target],
        ),
        out_shape=[out, out],
        compiler_params=pltpu.CompilerParams(vmem_limit_bytes=24 << 20),
        name="place_columns",
    )(slots, sums)


def swap(value, bit, node_count):
    return lax.ppermute(value, "node", [(i, i ^ bit) for i in range(node_count)])


def halved(wavefunctions, h_wavefunctions, block_ids):
    local_states = wavefunctions.shape[1]
    node_count = lax.axis_size("node")
    share_rows = local_states // node_count
    local_blocks = local_states // BLOCK
    node = lax.axis_index("node")
    state = lax.axis_index("state")

    owned = block_ids // local_blocks == state
    owned_count = jnp.sum(owned.astype(jnp.int32))
    order = jnp.argsort(jnp.logical_not(owned), stable=True).astype(jnp.int32)
    places = (block_ids % local_blocks)[order]
    own = block_columns(wavefunctions, h_wavefunctions, places[: NBLK - 1])
    other = lax.ppermute(own, "state", [(0, 1), (1, 0)])
    first = own[0]
    rest = jnp.concatenate(
        [
            jnp.where(
                i < owned_count,
                own[min(i, NBLK - 2)],
                lax.dynamic_index_in_dim(other, jnp.clip(i - owned_count, 0, NBLK - 2), 0, False),
            )
            for i in range(1, NBLK)
        ]
    )

    sums = []
    start = 0
    for bits, width in PARTS:
        if start < 2 * BLOCK:
            columns = first[start : start + width]
        else:
            columns = rest[start - 2 * BLOCK : start - 2 * BLOCK + width]
        start += width
        values = [BITS[b] for b in bits]
        groups = [
            sum(v for k, v in enumerate(values) if r >> (len(bits) - 1 - k) & 1) for r in range(node_count)
        ]
        half = node_count // 2
        groups = jnp.bitwise_xor(jnp.array(groups, jnp.int32), node)
        sent = partial_sums(wavefunctions, columns, groups[half:], share_rows)
        kept = [partial_sums(wavefunctions, columns, groups[:half], share_rows)]
        for value in values:
            kept.append(swap(sent, value, node_count))
            half = half // 2
            if half:
                sent = sum(k[half : 2 * half] for k in reversed(kept))
        sums.append(sum(k[0] for k in reversed(kept)))
    sums = jnp.concatenate(sums).reshape(NBLK, 2 * BLOCK, share_rows)
    return tuple(place_columns(sums, order, share_rows))


def gathered(wavefunctions, h_wavefunctions, block_ids):
    local_states = wavefunctions.shape[1]
    state = lax.axis_index("state")
    columns = []
    for step in range(NBLK):
        first = block_ids[step] * BLOCK
        owner = first // local_states
        offset = first - owner * local_states
        for array in (wavefunctions, h_wavefunctions):
            block = lax.dynamic_slice_in_dim(array, offset, BLOCK, 1)
            columns.append(jnp.where(state == owner, block, 0))
    columns = columns[::2] + columns[1::2]
    columns = lax.psum(jnp.concatenate(columns, axis=1), "state")
    full = jnp.dot(
        wavefunctions.T, columns, preferred_element_type=jnp.float32, precision=lax.Precision.HIGH
    )
    mine = lax.psum_scatter(full, "node", scatter_dimension=0, tiled=True)
    return mine[:, : NBLK * BLOCK], mine[:, NBLK * BLOCK :]


def solution(mesh):
    node_count, state_count = mesh.shape["node"], mesh.shape["state"]

    def body(wavefunctions, h_wavefunctions, block_ids):
        share_rows = wavefunctions.shape[1] // node_count
        fits = node_count == 16 and state_count == 2 and share_rows % LANES == 0
        return (halved if fits else gathered)(wavefunctions, h_wavefunctions, block_ids)

    placed = (P("node", "state"), P("node", "state"), P())
    return jax.shard_map(
        body,
        mesh=mesh,
        in_specs=placed,
        out_specs=(P(("state", "node"), None), P(("state", "node"), None)),
        check_vma=False,
    )
```

```python
import functools

import jax
import jax.numpy as jnp
from jax import lax
from jax.experimental import pallas as pl
from jax.experimental.pallas import tpu as pltpu
from jax.sharding import PartitionSpec as P

BLOCK = 128
NBLK = 4
LANES = 128
BUFFERS = 4
STEPS = 8
VMEM = 50 << 20

BITS = {"x": 1, "y": 2, "z": 4, "w": 8}

GROUPS = (
    (("xyzw", 88), ("yxzw", 88), ("zxyw", 80)),
    (("xyzw", 128), ("yxzw", 136), ("zyxw", 120)),
    (("xyzw", 136), ("yxzw", 128), ("zxyw", 120)),
)

ORDER = ("0", "1", 0, 1, 2, "2", 0, 1, 2, 3, 4, 5, 0, 1, 2, 3, 4, 5, 6, 7, 8, 3, 4, 5, 6, 7, 8, 6, 7, 8)


def split(value):
    high = value.astype(jnp.bfloat16)
    low = (value - high.astype(jnp.float32)).astype(jnp.bfloat16)
    return high, low


def ranked(info, rank, local_blocks):
    owned = [(lax.div(info[i], local_blocks) == info[NBLK + 1]).astype(jnp.int32) for i in range(NBLK)]
    mine = sum(owned)
    place, slot = 0, 0
    for i in range(NBLK):
        at = jnp.where(owned[i] == 1, sum(owned[:i]), mine + i - sum(owned[:i]))
        place = jnp.where(at == rank, lax.rem(info[i], local_blocks), place)
        slot = jnp.where(at == rank, i, slot)
    return place, slot


def owned_count(info, local_blocks):
    return sum((lax.div(info[i], local_blocks) == info[NBLK + 1]).astype(jnp.int32) for i in range(NBLK))


def columns_kernel(info, psi_ref, hpsi_ref, out_ref):
    out_ref[0, :BLOCK, :] = psi_ref[...].T
    out_ref[0, BLOCK:, :] = hpsi_ref[...].T


def block_columns(wavefunctions, h_wavefunctions, info, local_blocks):
    nodes = wavefunctions.shape[0]
    count = NBLK - 1
    source = pl.BlockSpec((nodes, BLOCK), lambda i, info: (0, ranked(info, i, local_blocks)[0]))
    return pl.pallas_call(
        columns_kernel,
        grid_spec=pltpu.PrefetchScalarGridSpec(
            num_scalar_prefetch=1,
            grid=(count,),
            in_specs=[source, source],
            out_specs=pl.BlockSpec((1, 2 * BLOCK, nodes), lambda i, info: (i, 0, 0)),
        ),
        out_shape=jax.ShapeDtypeStruct((count, 2 * BLOCK, nodes), jnp.float32),
        compiler_params=pltpu.CompilerParams(vmem_limit_bytes=VMEM),
        cost_estimate=pl.CostEstimate(
            flops=0, bytes_accessed=count * 4 * BLOCK * nodes * 4, transcendentals=0
        ),
        name="block_columns",
    )(info, wavefunctions, h_wavefunctions)


def bit_of(step, axis):
    shift = {"y": 2, "z": 1, "w": 0}[axis]
    return (step >> shift) & 1


def taken(step, axis, sent):
    bit = {"y": 4, "z": 2, "w": 1}[axis]
    before = step & -(2 * bit)
    if sent:
        return jnp.where(step & bit, step, jnp.maximum(before - 1, bit))
    return jnp.where(step & bit, before + bit - 1, step)


def partial_kernel(info, own_ref, other_ref, states_ref, token_ref, *refs, outs, pieces, local_blocks):
    del token_ref
    out_refs, (columns_ref, stack_ref, block_ref, columns_sem, sem) = refs[: len(outs)], refs[len(outs) :]
    width = columns_ref.shape[0]
    share_rows = block_ref.shape[2] // 2
    step = pl.program_id(0)
    slot = step % BUFFERS

    def fetch(at):
        copies = []
        for half in range(2):
            relative = (bit_of(at, "y") << 1) | (bit_of(at, "z") << 2) | (bit_of(at, "w") << 3) | half
            group = relative ^ info[NBLK]
            copies.append(
                pltpu.make_async_copy(
                    states_ref.at[:, pl.ds(pl.multiple_of(group * share_rows, share_rows), share_rows)],
                    block_ref.at[at % BUFFERS, :, pl.ds(half * share_rows, share_rows)],
                    sem.at[at % BUFFERS, half],
                )
            )
        return copies

    @pl.when(step == 0)
    def _():
        for ahead in range(BUFFERS - 1):
            for copy in fetch(ahead):
                copy.start()
        mine = owned_count(info, local_blocks)
        row = 0
        for number, (rank, first, rows) in enumerate(pieces):
            here = columns_ref.at[pl.ds(row, rows)]
            row += rows

            @pl.when(rank < mine)
            def _():
                source = own_ref.at[min(rank, NBLK - 2), pl.ds(first, rows)]
                pltpu.make_async_copy(source, here, columns_sem.at[number]).start()

            @pl.when(rank >= mine)
            def _():
                source = other_ref.at[jnp.clip(rank - mine, 0, NBLK - 2), pl.ds(first, rows)]
                pltpu.make_async_copy(source, here, columns_sem.at[number]).start()

        row = 0
        for number, (rank, first, rows) in enumerate(pieces):
            here = columns_ref.at[pl.ds(row, rows)]
            row += rows
            pltpu.make_async_copy(here, here, columns_sem.at[number]).wait()
        stack_ref[:width], stack_ref[width:] = split(columns_ref[...])

    @pl.when(step + BUFFERS - 1 < STEPS)
    def _():
        for copy in fetch(step + BUFFERS - 1):
            copy.start()

    for copy in fetch(step):
        copy.wait()
    dot = functools.partial(jnp.dot, preferred_element_type=jnp.float32)
    high, low = split(block_ref[slot])
    both = dot(stack_ref[...], high)
    result = both[:width] + (both[width:] + dot(stack_ref[:width], low))
    halves = (result[:, :share_rows], result[:, share_rows:])
    for (bits, start, size, sent), out_ref in zip(outs, out_refs):
        if bits[0] == "x":
            out_ref[0, 0, 0] = halves[sent][start : start + size]
            continue
        at = bits.index("x") - 1

        @pl.when(bit_of(step, bits[0]) == sent)
        def _():
            for half in range(2):
                index = tuple(half if k == at else 0 for k in range(3))
                out_ref[index] = halves[half][start : start + size]


def partial_sums(wavefunctions, own, other, info, share_rows, parts, first, token):
    nodes = wavefunctions.shape[0]
    width = sum(size for _, size in parts)
    outs = []
    for sent in (1, 0):
        start = 0
        for bits, size in parts:
            outs.append((bits, start, size, sent))
            start += size
    pieces = []
    at = first
    while at < first + width:
        rank, row = divmod(at, 2 * BLOCK)
        rows = min(2 * BLOCK - row, first + width - at)
        pieces.append((rank, row, rows))
        at += rows

    def spec(bits, start, size, sent):
        def index(step, info):
            if bits[0] != "x":
                step = taken(step, bits[0], sent)
            return (*(0 if b == "x" else bit_of(step, b) for b in bits[1:]), 0, 0)

        return pl.BlockSpec((*(2 if b == "x" else 1 for b in bits[1:]), size, share_rows), index)

    made = pl.pallas_call(
        functools.partial(
            partial_kernel, outs=outs, pieces=pieces, local_blocks=wavefunctions.shape[1] // BLOCK
        ),
        grid_spec=pltpu.PrefetchScalarGridSpec(
            num_scalar_prefetch=1,
            grid=(STEPS,),
            in_specs=[pl.BlockSpec(memory_space=pl.ANY)] * 4,
            out_specs=[spec(*out) for out in outs],
            scratch_shapes=[
                pltpu.VMEM((width, nodes), jnp.float32),
                pltpu.VMEM((2 * width, nodes), jnp.bfloat16),
                pltpu.VMEM((BUFFERS, nodes, 2 * share_rows), jnp.float32),
                pltpu.SemaphoreType.DMA((len(pieces),)),
                pltpu.SemaphoreType.DMA((BUFFERS, 2)),
            ],
        ),
        out_shape=[jax.ShapeDtypeStruct((2, 2, 2, out[2], share_rows), jnp.float32) for out in outs],
        compiler_params=pltpu.CompilerParams(vmem_limit_bytes=VMEM),
        cost_estimate=pl.CostEstimate(
            flops=12 * STEPS * width * share_rows * nodes,
            bytes_accessed=8 * STEPS * share_rows * (nodes + width),
            transcendentals=0,
        ),
        name="partial_sums",
    )(info, own, other, wavefunctions, token)
    return [m.reshape(8, *m.shape[3:]) for m in made]


def total(leaves, at):
    value = leaves[0][at]
    for leaf in leaves[1:]:
        value = value + leaf[at]
    return value


def add_kernel(*refs):
    refs[-1][0] = total(refs[:-2], 0)


def add_up(leaves, count, token):
    shape = leaves[0].shape[1:]
    return pl.pallas_call(
        add_kernel,
        grid=(count,),
        in_specs=[pl.BlockSpec((1, *shape), lambda i: (count + i, 0, 0))] * len(leaves)
        + [pl.BlockSpec(memory_space=pl.ANY)],
        out_specs=pl.BlockSpec((1, *shape), lambda i: (i, 0, 0)),
        out_shape=jax.ShapeDtypeStruct((count, *shape), jnp.float32),
        compiler_params=pltpu.CompilerParams(vmem_limit_bytes=16 << 20),
        cost_estimate=pl.CostEstimate(
            flops=0, bytes_accessed=4 * count * shape[0] * shape[1] * (len(leaves) + 1), transcendentals=0
        ),
        name="add_up",
    )(*leaves, token)


def place_kernel(info, sums_ref, correlation_ref, energy_ref):
    correlation_ref[...] = sums_ref[0, :BLOCK, :].T
    energy_ref[...] = sums_ref[0, BLOCK:, :].T


def place_columns(sums, info, share_rows, local_blocks):
    out = jax.ShapeDtypeStruct((share_rows, NBLK * BLOCK), jnp.float32)
    target = pl.BlockSpec((share_rows, BLOCK), lambda i, info: (0, ranked(info, i, local_blocks)[1]))
    return pl.pallas_call(
        place_kernel,
        grid_spec=pltpu.PrefetchScalarGridSpec(
            num_scalar_prefetch=1,
            grid=(NBLK,),
            in_specs=[pl.BlockSpec((1, 2 * BLOCK, share_rows), lambda i, info: (i, 0, 0))],
            out_specs=[target, target],
        ),
        out_shape=[out, out],
        compiler_params=pltpu.CompilerParams(vmem_limit_bytes=24 << 20),
        name="place_columns",
    )(info, sums)


def swap(value, axis):
    bit = BITS[axis]
    return lax.ppermute(value, "node", [(i, i ^ bit) for i in range(lax.axis_size("node"))])


def swap_cores(value):
    return lax.ppermute(value, "state", [(0, 1), (1, 0)])


def other_columns(first, more, other, owned_count):
    own, other = jnp.concatenate([first, more]), jnp.concatenate(other)
    return jnp.concatenate(
        [
            jnp.where(
                i < owned_count,
                own[min(i, NBLK - 2)],
                lax.dynamic_index_in_dim(other, jnp.clip(i - owned_count, 0, NBLK - 2), 0, False),
            )
            for i in range(1, NBLK)
        ]
    )


def halved(wavefunctions, h_wavefunctions, block_ids):
    local_states = wavefunctions.shape[1]
    share_rows = local_states // lax.axis_size("node")
    local_blocks = local_states // BLOCK
    info = jnp.concatenate([block_ids, lax.axis_index("node")[None], lax.axis_index("state")[None]])

    own = block_columns(wavefunctions, h_wavefunctions, info, local_blocks)
    other = swap_cores(own)
    last = own
    held, sizes = {}, {}
    first = 0
    for step in ORDER:
        if isinstance(step, str):
            group = int(step)
            parts = GROUPS[group]
            out = partial_sums(
                wavefunctions, own, other if group else own, info, share_rows, parts, first, last
            )
            last = out[0]
            first += sum(size for _, size in parts)
            sent, kept = out[: len(parts)], out[len(parts) :]
            for (bits, size), send, keep in zip(parts, sent, kept):
                held[len(held)] = (bits, [keep, swap(send, bits[0])])
        else:
            bits, leaves = held[step]
            turn = len(leaves) - 1
            last = add_up(leaves, 8 >> turn, last)
            leaves.append(swap(last, bits[turn]))
    results = [total(leaves, 0) for _, leaves in held.values()]
    sums = jnp.concatenate(results).reshape(NBLK, 2 * BLOCK, share_rows)
    return tuple(place_columns(sums, info, share_rows, local_blocks))


def gathered(wavefunctions, h_wavefunctions, block_ids):
    local_states = wavefunctions.shape[1]
    state = lax.axis_index("state")
    columns = []
    for step in range(NBLK):
        first = block_ids[step] * BLOCK
        owner = first // local_states
        offset = first - owner * local_states
        for array in (wavefunctions, h_wavefunctions):
            block = lax.dynamic_slice_in_dim(array, offset, BLOCK, 1)
            columns.append(jnp.where(state == owner, block, 0))
    columns = columns[::2] + columns[1::2]
    columns = lax.psum(jnp.concatenate(columns, axis=1), "state")
    full = jnp.dot(
        wavefunctions.T, columns, preferred_element_type=jnp.float32, precision=lax.Precision.HIGH
    )
    mine = lax.psum_scatter(full, "node", scatter_dimension=0, tiled=True)
    return mine[:, : NBLK * BLOCK], mine[:, NBLK * BLOCK :]


def solution(mesh):
    node_count, state_count = mesh.shape["node"], mesh.shape["state"]

    def body(wavefunctions, h_wavefunctions, block_ids):
        share_rows = wavefunctions.shape[1] // node_count
        fits = node_count == 16 and state_count == 2 and share_rows % LANES == 0
        return (halved if fits else gathered)(wavefunctions, h_wavefunctions, block_ids)

    placed = (P("node", "state"), P("node", "state"), P())
    return jax.shard_map(
        body,
        mesh=mesh,
        in_specs=placed,
        out_specs=(P(("state", "node"), None), P(("state", "node"), None)),
        check_vma=False,
    )
```

```python
import functools

import jax
import jax.numpy as jnp
from jax import lax
from jax.experimental import pallas as pl
from jax.experimental.pallas import tpu as pltpu
from jax.sharding import PartitionSpec as P

BLOCK = 128
NBLK = 4
LANES = 128
BUFFERS = 4
STEPS = 8
VMEM = 50 << 20

BITS = {"x": 1, "y": 2, "z": 4, "w": 8}

GROUPS = (
    (("xyzw", 88), ("yxzw", 88), ("zwyx", 80)),
    (("xyzw", 128), ("yxzw", 136), ("zyxw", 120)),
    (("xyzw", 144), ("yxzw", 112), ("zxyw", 128)),
)

ORDER = (
    "0", "1", 0, 1, 2, "2", 0, 1, 3, 2, 3, 4, 5, 0, 1, 2, 4, 7, 5, 6, 8, 3, 4, 5, 6, 7, 8, 6, 8, 7,
)


def split(value):
    high = value.astype(jnp.bfloat16)
    low = (value - high.astype(jnp.float32)).astype(jnp.bfloat16)
    return high, low


def ranked(info, rank, local_blocks):
    owned = [(lax.div(info[i], local_blocks) == info[NBLK + 1]).astype(jnp.int32) for i in range(NBLK)]
    mine = sum(owned)
    place, slot = 0, 0
    for i in range(NBLK):
        at = jnp.where(owned[i] == 1, sum(owned[:i]), mine + i - sum(owned[:i]))
        place = jnp.where(at == rank, lax.rem(info[i], local_blocks), place)
        slot = jnp.where(at == rank, i, slot)
    return place, slot


def owned_count(info, local_blocks):
    return sum((lax.div(info[i], local_blocks) == info[NBLK + 1]).astype(jnp.int32) for i in range(NBLK))


def bit_of(step, axis):
    shift = {"y": 2, "z": 1, "w": 0}[axis]
    return (step >> shift) & 1


def taken(step, axis, sent):
    bit = {"y": 4, "z": 2, "w": 1}[axis]
    before = step & -(2 * bit)
    if sent:
        return jnp.where(step & bit, step, jnp.maximum(before - 1, bit))
    return jnp.where(step & bit, before + bit - 1, step)


def partial_kernel(info, *refs, outs, first, local_blocks):
    states_ref, refs = refs[0], refs[1:]
    if first == 0:
        source_refs, refs = refs[:1], refs[1:]
    else:
        source_refs, refs = refs[:2], refs[3:]
    out_refs, refs = refs[: len(outs)], refs[len(outs) :]
    if first == 0:
        own_ref, *refs, held_ref, held_sem, own_sem = refs
    columns_ref, stack_ref, block_ref, columns_sem, sem = refs
    blocks = columns_ref.shape[0]
    width = blocks * BLOCK
    share_rows = block_ref.shape[2] // 2
    step = pl.program_id(0)

    def fetch(at):
        copies = []
        for half in range(2):
            relative = (bit_of(at, "y") << 1) | (bit_of(at, "z") << 2) | (bit_of(at, "w") << 3) | half
            group = relative ^ info[NBLK]
            copies.append(
                pltpu.make_async_copy(
                    states_ref.at[:, pl.ds(pl.multiple_of(group * share_rows, share_rows), share_rows)],
                    block_ref.at[at % BUFFERS, :, pl.ds(half * share_rows, share_rows)],
                    sem.at[at % BUFFERS, half],
                )
            )
        return copies

    def gather(rank, which):
        place = ranked(info, rank, local_blocks)[0]
        columns = pl.ds(pl.multiple_of(place * BLOCK, BLOCK), BLOCK)
        source = (states_ref, source_refs[0])[which]
        return pltpu.make_async_copy(source.at[:, columns], held_ref.at[rank, which], held_sem.at[rank, which])

    def hand_over():
        return pltpu.make_async_copy(held_ref, own_ref, own_sem)

    @pl.when(step == 0)
    def _():
        mine = owned_count(info, local_blocks)
        for block in range(blocks):
            rank, which = divmod(first // BLOCK + block, 2)
            here, semaphore = columns_ref.at[block], columns_sem.at[block]

            def bring(source, at):
                pltpu.make_async_copy(source.at[at, which], here, semaphore).start()

            if first == 0:
                gather(rank, which).start()
            else:
                pl.when(rank < mine)(functools.partial(bring, source_refs[0], min(rank, NBLK - 2)))
                pl.when(rank >= mine)(
                    functools.partial(bring, source_refs[1], jnp.clip(rank - mine, 0, NBLK - 2))
                )
        for ahead in range(BUFFERS):
            for copy in fetch(ahead):
                copy.start()
        if first == 0:
            for block in range(blocks, 2 * (NBLK - 1)):
                gather(*divmod(block, 2)).start()
        for block in range(blocks):
            if first == 0:
                gather(*divmod(block, 2)).wait()
                columns = held_ref[block // 2, block % 2]
            else:
                here = columns_ref.at[block]
                pltpu.make_async_copy(here, here, columns_sem.at[block]).wait()
                columns = columns_ref[block]
            rows = pl.ds(block * BLOCK, BLOCK)
            low_rows = pl.ds(width + block * BLOCK, BLOCK)
            stack_ref[rows], stack_ref[low_rows] = split(columns.T)

    @pl.when((step >= 1) & (step + BUFFERS - 1 < STEPS))
    def _():
        for copy in fetch(step + BUFFERS - 1):
            copy.start()

    for copy in fetch(step):
        copy.wait()
    multiply(step, block_ref.at[step % BUFFERS], stack_ref, outs, out_refs)

    if first == 0:

        @pl.when(step == STEPS // 2)
        def _():
            for block in range(blocks, 2 * (NBLK - 1)):
                gather(*divmod(block, 2)).wait()
            hand_over().start()

        @pl.when(step == STEPS - 1)
        def _():
            hand_over().wait()


def multiply(step, block_ref, stack_ref, outs, out_refs):
    width = stack_ref.shape[0] // 2
    share_rows = block_ref.shape[1] // 2
    dot = functools.partial(jnp.dot, preferred_element_type=jnp.float32)
    high, low = split(block_ref[...])
    both = dot(stack_ref[...], high)
    result = both[:width] + (both[width:] + dot(stack_ref[:width], low))
    halves = (result[:, :share_rows], result[:, share_rows:])
    for (bits, start, size, sent), out_ref in zip(outs, out_refs):
        if bits[0] == "x":
            out_ref[0, 0, 0] = halves[sent][start : start + size]
            continue
        at = bits.index("x") - 1

        @pl.when(bit_of(step, bits[0]) == sent)
        def _():
            for half in range(2):
                index = tuple(half if k == at else 0 for k in range(3))
                out_ref[index] = halves[half][start : start + size]


def partial_sums(wavefunctions, sources, info, share_rows, parts, first):
    nodes = wavefunctions.shape[0]
    width = sum(size for _, size in parts)
    outs = []
    for sent in (1, 0):
        start = 0
        for bits, size in parts:
            outs.append((bits, start, size, sent))
            start += size

    def spec(bits, start, size, sent):
        def index(step, info):
            if bits[0] != "x":
                step = taken(step, bits[0], sent)
            return (*(0 if b == "x" else bit_of(step, b) for b in bits[1:]), 0, 0)

        return pl.BlockSpec((*(2 if b == "x" else 1 for b in bits[1:]), size, share_rows), index)

    columns = []
    if first == 0:
        columns = [jax.ShapeDtypeStruct((NBLK - 1, 2, nodes, BLOCK), jnp.float32)]
    made = pl.pallas_call(
        functools.partial(
            partial_kernel,
            outs=outs,
            first=first,
            local_blocks=wavefunctions.shape[1] // BLOCK,
        ),
        grid_spec=pltpu.PrefetchScalarGridSpec(
            num_scalar_prefetch=1,
            grid=(STEPS,),
            in_specs=[pl.BlockSpec(memory_space=pl.ANY)] * (len(sources) + 1),
            out_specs=[spec(*out) for out in outs] + [pl.BlockSpec(memory_space=pl.ANY)] * len(columns),
            scratch_shapes=[
                pltpu.VMEM((width // BLOCK, nodes, BLOCK), jnp.float32),
                pltpu.VMEM((2 * width, nodes), jnp.bfloat16),
                pltpu.VMEM((BUFFERS, nodes, 2 * share_rows), jnp.float32),
                pltpu.SemaphoreType.DMA((width // BLOCK,)),
                pltpu.SemaphoreType.DMA((BUFFERS, 2)),
            ]
            + [
                scratch
                for shape in columns
                for scratch in (
                    pltpu.VMEM(shape.shape, shape.dtype),
                    pltpu.SemaphoreType.DMA((NBLK - 1, 2)),
                    pltpu.SemaphoreType.DMA,
                )
            ],
        ),
        out_shape=[jax.ShapeDtypeStruct((2, 2, 2, out[2], share_rows), jnp.float32) for out in outs] + columns,
        compiler_params=pltpu.CompilerParams(vmem_limit_bytes=VMEM),
        cost_estimate=pl.CostEstimate(
            flops=12 * STEPS * width * share_rows * nodes,
            bytes_accessed=8 * STEPS * share_rows * (nodes + width),
            transcendentals=0,
        ),
        name="partial_sums",
    )(info, wavefunctions, *sources)
    return [m.reshape(8, *m.shape[3:]) for m in made[: len(outs)]] + list(made[len(outs) :])


def total(leaves, at):
    value = leaves[0][at]
    for leaf in leaves[1:]:
        value = value + leaf[at]
    return value


def add_kernel(*refs):
    refs[-1][0] = total(refs[:-2], 0)


def add_up(leaves, count, token):
    shape = leaves[0].shape[1:]
    return pl.pallas_call(
        add_kernel,
        grid=(count,),
        in_specs=[pl.BlockSpec((1, *shape), lambda i: (count + i, 0, 0))] * len(leaves)
        + [pl.BlockSpec(memory_space=pl.ANY)],
        out_specs=pl.BlockSpec((1, *shape), lambda i: (i, 0, 0)),
        out_shape=jax.ShapeDtypeStruct((count, *shape), jnp.float32),
        compiler_params=pltpu.CompilerParams(vmem_limit_bytes=16 << 20),
        cost_estimate=pl.CostEstimate(
            flops=0, bytes_accessed=4 * count * shape[0] * shape[1] * (len(leaves) + 1), transcendentals=0
        ),
        name="add_up",
    )(*leaves, token)


def place_kernel(info, sums_ref, correlation_ref, energy_ref):
    correlation_ref[...] = sums_ref[0, :BLOCK, :].T
    energy_ref[...] = sums_ref[0, BLOCK:, :].T


def place_columns(sums, info, share_rows, local_blocks):
    out = jax.ShapeDtypeStruct((share_rows, NBLK * BLOCK), jnp.float32)
    target = pl.BlockSpec((share_rows, BLOCK), lambda i, info: (0, ranked(info, i, local_blocks)[1]))
    return pl.pallas_call(
        place_kernel,
        grid_spec=pltpu.PrefetchScalarGridSpec(
            num_scalar_prefetch=1,
            grid=(NBLK,),
            in_specs=[pl.BlockSpec((1, 2 * BLOCK, share_rows), lambda i, info: (i, 0, 0))],
            out_specs=[target, target],
        ),
        out_shape=[out, out],
        compiler_params=pltpu.CompilerParams(vmem_limit_bytes=24 << 20),
        name="place_columns",
    )(info, sums)


def swap(value, axis):
    bit = BITS[axis]
    return lax.ppermute(value, "node", [(i, i ^ bit) for i in range(lax.axis_size("node"))])


def swap_cores(value):
    return lax.ppermute(value, "state", [(0, 1), (1, 0)])


def other_columns(first, more, other, owned_count):
    own, other = jnp.concatenate([first, more]), jnp.concatenate(other)
    return jnp.concatenate(
        [
            jnp.where(
                i < owned_count,
                own[min(i, NBLK - 2)],
                lax.dynamic_index_in_dim(other, jnp.clip(i - owned_count, 0, NBLK - 2), 0, False),
            )
            for i in range(1, NBLK)
        ]
    )


def halved(wavefunctions, h_wavefunctions, block_ids):
    local_states = wavefunctions.shape[1]
    share_rows = local_states // lax.axis_size("node")
    local_blocks = local_states // BLOCK
    info = jnp.concatenate([block_ids, lax.axis_index("node")[None], lax.axis_index("state")[None]])

    held = {}
    first = 0
    for step in ORDER:
        if isinstance(step, str):
            group = int(step)
            parts = GROUPS[group]
            sources = [own, other, last] if group else [h_wavefunctions]
            out = partial_sums(wavefunctions, sources, info, share_rows, parts, first)
            last = out[0]
            if group == 0:
                own = out.pop()
                other = swap_cores(own)
            first += sum(size for _, size in parts)
            sent, kept = out[: len(parts)], out[len(parts) :]
            for (bits, size), send, keep in zip(parts, sent, kept):
                held[len(held)] = (bits, [keep, swap(send, bits[0])])
        else:
            bits, leaves = held[step]
            turn = len(leaves) - 1
            last = add_up(leaves, 8 >> turn, last)
            leaves.append(swap(last, bits[turn]))
    results = [total(leaves, 0) for _, leaves in held.values()]
    sums = jnp.concatenate(results).reshape(NBLK, 2 * BLOCK, share_rows)
    return tuple(place_columns(sums, info, share_rows, local_blocks))


def gathered(wavefunctions, h_wavefunctions, block_ids):
    local_states = wavefunctions.shape[1]
    state = lax.axis_index("state")
    columns = []
    for step in range(NBLK):
        first = block_ids[step] * BLOCK
        owner = first // local_states
        offset = first - owner * local_states
        for array in (wavefunctions, h_wavefunctions):
            block = lax.dynamic_slice_in_dim(array, offset, BLOCK, 1)
            columns.append(jnp.where(state == owner, block, 0))
    columns = columns[::2] + columns[1::2]
    columns = lax.psum(jnp.concatenate(columns, axis=1), "state")
    full = jnp.dot(
        wavefunctions.T, columns, preferred_element_type=jnp.float32, precision=lax.Precision.HIGH
    )
    mine = lax.psum_scatter(full, "node", scatter_dimension=0, tiled=True)
    return mine[:, : NBLK * BLOCK], mine[:, NBLK * BLOCK :]


def solution(mesh):
    node_count, state_count = mesh.shape["node"], mesh.shape["state"]

    def body(wavefunctions, h_wavefunctions, block_ids):
        share_rows = wavefunctions.shape[1] // node_count
        fits = node_count == 16 and state_count == 2 and share_rows % LANES == 0
        return (halved if fits else gathered)(wavefunctions, h_wavefunctions, block_ids)

    placed = (P("node", "state"), P("node", "state"), P())
    return jax.shard_map(
        body,
        mesh=mesh,
        in_specs=placed,
        out_specs=(P(("state", "node"), None), P(("state", "node"), None)),
        check_vma=False,
    )
```

```python
import functools

import jax
import jax.numpy as jnp
from jax import lax
from jax.experimental import pallas as pl
from jax.experimental.pallas import tpu as pltpu
from jax.sharding import PartitionSpec as P

BLOCK = 128
NBLK = 4
LANES = 128
BUFFERS = 4
STEPS = 8
FLOPS = 115_000_000
VMEM = 50 << 20

BITS = {"x": 1, "y": 2, "z": 4, "w": 8}

GROUPS = (
    (("yzxw", 136), ("xzyw", 120)),
    (("yzxw", 104), ("xyzw", 144), ("xzwy", 136)),
    (("yzxw", 176), ("zyxw", 104), ("xyzw", 104)),
)

ORDER = (
    ("0", 50), ("1", 70), (1, 6), (0, 3), ("2", 52), (1, 3), (2, 13), (0, 3), (3, 5), (1, 18), (0, 3),
    (2, 21), (3, 3), (2, 25), (3, 48), (4, 14), (6, 21), (5, 17), (4, 6), (7, 6), (6, 22), (6, 8), (7, 3),
    (4, 3), (5, 20), (7, 12), (5, 6),
)


def split(value):
    high = value.astype(jnp.bfloat16)
    low = (value - high.astype(jnp.float32)).astype(jnp.bfloat16)
    return high, low


def ranked(info, rank, local_blocks):
    owned = [(lax.div(info[i], local_blocks) == info[NBLK + 1]).astype(jnp.int32) for i in range(NBLK)]
    mine = sum(owned)
    place, slot = 0, 0
    for i in range(NBLK):
        at = jnp.where(owned[i] == 1, sum(owned[:i]), mine + i - sum(owned[:i]))
        place = jnp.where(at == rank, lax.rem(info[i], local_blocks), place)
        slot = jnp.where(at == rank, i, slot)
    return place, slot


def owned_count(info, local_blocks):
    return sum((lax.div(info[i], local_blocks) == info[NBLK + 1]).astype(jnp.int32) for i in range(NBLK))


def bit_of(step, axis):
    shift = {"y": 2, "z": 1, "w": 0}[axis]
    return (step >> shift) & 1


def taken(step, axis, sent):
    bit = {"y": 4, "z": 2, "w": 1}[axis]
    before = step & -(2 * bit)
    if sent:
        return jnp.where(step & bit, step, jnp.maximum(before - 1, bit))
    return jnp.where(step & bit, before + bit - 1, step)


def partial_kernel(info, *refs, outs, first, local_blocks):
    states_ref, refs = refs[0], refs[1:]
    if first == 0:
        source_refs, refs = refs[:1], refs[1:]
    else:
        source_refs, refs = refs[:2], refs[3:]
    out_refs, refs = refs[: len(outs)], refs[len(outs) :]
    if first == 0:
        own_ref, *refs, held_ref, held_sem, own_sem = refs
    columns_ref, stack_ref, block_ref, columns_sem, sem = refs
    blocks = columns_ref.shape[0]
    width = blocks * BLOCK
    share_rows = block_ref.shape[2] // 2
    step = pl.program_id(0)

    def fetch(at):
        copies = []
        for half in range(2):
            relative = (bit_of(at, "y") << 1) | (bit_of(at, "z") << 2) | (bit_of(at, "w") << 3) | half
            group = relative ^ info[NBLK]
            copies.append(
                pltpu.make_async_copy(
                    states_ref.at[:, pl.ds(pl.multiple_of(group * share_rows, share_rows), share_rows)],
                    block_ref.at[at % BUFFERS, :, pl.ds(half * share_rows, share_rows)],
                    sem.at[at % BUFFERS, half],
                )
            )
        return copies

    def gather(rank, which):
        place = ranked(info, rank, local_blocks)[0]
        columns = pl.ds(pl.multiple_of(place * BLOCK, BLOCK), BLOCK)
        source = (states_ref, source_refs[0])[which]
        return pltpu.make_async_copy(source.at[:, columns], held_ref.at[rank, which], held_sem.at[rank, which])

    def hand_over():
        return pltpu.make_async_copy(held_ref, own_ref, own_sem)

    @pl.when(step == 0)
    def _():
        mine = owned_count(info, local_blocks)
        for block in range(blocks):
            rank, which = divmod(first // BLOCK + block, 2)
            here, semaphore = columns_ref.at[block], columns_sem.at[block]

            def bring(source, at):
                pltpu.make_async_copy(source.at[at, which], here, semaphore).start()

            if first == 0:
                gather(rank, which).start()
            else:
                pl.when(rank < mine)(functools.partial(bring, source_refs[0], min(rank, NBLK - 2)))
                pl.when(rank >= mine)(
                    functools.partial(bring, source_refs[1], jnp.clip(rank - mine, 0, NBLK - 2))
                )
        for ahead in range(BUFFERS):
            for copy in fetch(ahead):
                copy.start()
        if first == 0:
            for block in range(blocks, 2 * (NBLK - 1)):
                gather(*divmod(block, 2)).start()
        for block in range(blocks):
            if first == 0:
                gather(*divmod(block, 2)).wait()
                columns = held_ref[block // 2, block % 2]
            else:
                here = columns_ref.at[block]
                pltpu.make_async_copy(here, here, columns_sem.at[block]).wait()
                columns = columns_ref[block]
            rows = pl.ds(block * BLOCK, BLOCK)
            low_rows = pl.ds(width + block * BLOCK, BLOCK)
            stack_ref[rows], stack_ref[low_rows] = split(columns.T)

    @pl.when((step >= 1) & (step + BUFFERS - 1 < STEPS))
    def _():
        for copy in fetch(step + BUFFERS - 1):
            copy.start()

    for copy in fetch(step):
        copy.wait()
    multiply(step, block_ref.at[step % BUFFERS], stack_ref, outs, out_refs)

    if first == 0:

        @pl.when(step == STEPS // 2)
        def _():
            for block in range(blocks, 2 * (NBLK - 1)):
                gather(*divmod(block, 2)).wait()
            hand_over().start()

        @pl.when(step == STEPS - 1)
        def _():
            hand_over().wait()


def multiply(step, block_ref, stack_ref, outs, out_refs):
    width = stack_ref.shape[0] // 2
    share_rows = block_ref.shape[1] // 2
    dot = functools.partial(jnp.dot, preferred_element_type=jnp.float32)
    high, low = split(block_ref[...])
    both = dot(stack_ref[...], high)
    result = both[:width] + (both[width:] + dot(stack_ref[:width], low))
    halves = (result[:, :share_rows], result[:, share_rows:])
    for (bits, start, size, sent), out_ref in zip(outs, out_refs):
        if bits[0] == "x":
            out_ref[0, 0, 0] = halves[sent][start : start + size]
            continue
        at = bits.index("x") - 1

        @pl.when(bit_of(step, bits[0]) == sent)
        def _():
            for half in range(2):
                index = tuple(half if k == at else 0 for k in range(3))
                out_ref[index] = halves[half][start : start + size]


def partial_sums(wavefunctions, sources, info, share_rows, parts, first, beside):
    nodes = wavefunctions.shape[0]
    width = sum(size for _, size in parts)
    outs = []
    for sent in (1, 0):
        start = 0
        for bits, size in parts:
            outs.append((bits, start, size, sent))
            start += size

    def spec(bits, start, size, sent):
        def index(step, info):
            if bits[0] != "x":
                step = taken(step, bits[0], sent)
            return (*(0 if b == "x" else bit_of(step, b) for b in bits[1:]), 0, 0)

        return pl.BlockSpec((*(2 if b == "x" else 1 for b in bits[1:]), size, share_rows), index)

    columns = []
    if first == 0:
        columns = [jax.ShapeDtypeStruct((NBLK - 1, 2, nodes, BLOCK), jnp.float32)]
    made = pl.pallas_call(
        functools.partial(
            partial_kernel,
            outs=outs,
            first=first,
            local_blocks=wavefunctions.shape[1] // BLOCK,
        ),
        grid_spec=pltpu.PrefetchScalarGridSpec(
            num_scalar_prefetch=1,
            grid=(STEPS,),
            in_specs=[pl.BlockSpec(memory_space=pl.ANY)] * (len(sources) + 1),
            out_specs=[spec(*out) for out in outs] + [pl.BlockSpec(memory_space=pl.ANY)] * len(columns),
            scratch_shapes=[
                pltpu.VMEM((width // BLOCK, nodes, BLOCK), jnp.float32),
                pltpu.VMEM((2 * width, nodes), jnp.bfloat16),
                pltpu.VMEM((BUFFERS, nodes, 2 * share_rows), jnp.float32),
                pltpu.SemaphoreType.DMA((width // BLOCK,)),
                pltpu.SemaphoreType.DMA((BUFFERS, 2)),
            ]
            + [
                scratch
                for shape in columns
                for scratch in (
                    pltpu.VMEM(shape.shape, shape.dtype),
                    pltpu.SemaphoreType.DMA((NBLK - 1, 2)),
                    pltpu.SemaphoreType.DMA,
                )
            ],
        ),
        out_shape=[jax.ShapeDtypeStruct((2, 2, 2, out[2], share_rows), jnp.float32) for out in outs] + columns,
        compiler_params=pltpu.CompilerParams(vmem_limit_bytes=VMEM),
        cost_estimate=pl.CostEstimate(
            flops=beside * FLOPS,
            bytes_accessed=8 * STEPS * share_rows * (nodes + width),
            transcendentals=0,
        ),
        name="partial_sums",
    )(info, wavefunctions, *sources)
    return [m.reshape(8, *m.shape[3:]) for m in made[: len(outs)]] + list(made[len(outs) :])


def total(leaves, at):
    value = leaves[0][at]
    for leaf in leaves[1:]:
        value = value + leaf[at]
    return value


def add_kernel(*refs):
    refs[-1][0] = total(refs[:-2], 0)


def add_up(leaves, count, token, beside):
    shape = leaves[0].shape[1:]
    return pl.pallas_call(
        add_kernel,
        grid=(count,),
        in_specs=[pl.BlockSpec((1, *shape), lambda i: (count + i, 0, 0))] * len(leaves)
        + [pl.BlockSpec(memory_space=pl.ANY)],
        out_specs=pl.BlockSpec((1, *shape), lambda i: (i, 0, 0)),
        out_shape=jax.ShapeDtypeStruct((count, *shape), jnp.float32),
        compiler_params=pltpu.CompilerParams(vmem_limit_bytes=16 << 20),
        cost_estimate=pl.CostEstimate(
            flops=beside * FLOPS,
            bytes_accessed=4 * count * shape[0] * shape[1] * (len(leaves) + 1),
            transcendentals=0,
        ),
        name="add_up",
    )(*leaves, token)


def place_kernel(info, sums_ref, correlation_ref, energy_ref):
    correlation_ref[...] = sums_ref[0, :BLOCK, :].T
    energy_ref[...] = sums_ref[0, BLOCK:, :].T


def place_columns(sums, info, share_rows, local_blocks):
    out = jax.ShapeDtypeStruct((share_rows, NBLK * BLOCK), jnp.float32)
    target = pl.BlockSpec((share_rows, BLOCK), lambda i, info: (0, ranked(info, i, local_blocks)[1]))
    return pl.pallas_call(
        place_kernel,
        grid_spec=pltpu.PrefetchScalarGridSpec(
            num_scalar_prefetch=1,
            grid=(NBLK,),
            in_specs=[pl.BlockSpec((1, 2 * BLOCK, share_rows), lambda i, info: (i, 0, 0))],
            out_specs=[target, target],
        ),
        out_shape=[out, out],
        compiler_params=pltpu.CompilerParams(vmem_limit_bytes=24 << 20),
        name="place_columns",
    )(info, sums)


def swap(value, axis):
    bit = BITS[axis]
    return lax.ppermute(value, "node", [(i, i ^ bit) for i in range(lax.axis_size("node"))])


def swap_cores(value):
    return lax.ppermute(value, "state", [(0, 1), (1, 0)])


def other_columns(first, more, other, owned_count):
    own, other = jnp.concatenate([first, more]), jnp.concatenate(other)
    return jnp.concatenate(
        [
            jnp.where(
                i < owned_count,
                own[min(i, NBLK - 2)],
                lax.dynamic_index_in_dim(other, jnp.clip(i - owned_count, 0, NBLK - 2), 0, False),
            )
            for i in range(1, NBLK)
        ]
    )


def halved(wavefunctions, h_wavefunctions, block_ids):
    local_states = wavefunctions.shape[1]
    share_rows = local_states // lax.axis_size("node")
    local_blocks = local_states // BLOCK
    info = jnp.concatenate([block_ids, lax.axis_index("node")[None], lax.axis_index("state")[None]])

    held = {}
    first = 0
    for step, beside in ORDER:
        if isinstance(step, str):
            group = int(step)
            parts = GROUPS[group]
            sources = [own, other, last] if group else [h_wavefunctions]
            out = partial_sums(wavefunctions, sources, info, share_rows, parts, first, beside)
            last = out[0]
            if group == 0:
                own = out.pop()
                other = swap_cores(own)
            first += sum(size for _, size in parts)
            sent, kept = out[: len(parts)], out[len(parts) :]
            for (bits, size), send, keep in zip(parts, sent, kept):
                held[len(held)] = (bits, [keep, swap(send, bits[0])])
        else:
            bits, leaves = held[step]
            turn = len(leaves) - 1
            last = add_up(leaves, 8 >> turn, last, beside)
            leaves.append(swap(last, bits[turn]))
    results = [total(leaves, 0) for _, leaves in held.values()]
    sums = jnp.concatenate(results).reshape(NBLK, 2 * BLOCK, share_rows)
    return tuple(place_columns(sums, info, share_rows, local_blocks))


def gathered(wavefunctions, h_wavefunctions, block_ids):
    local_states = wavefunctions.shape[1]
    state = lax.axis_index("state")
    columns = []
    for step in range(NBLK):
        first = block_ids[step] * BLOCK
        owner = first // local_states
        offset = first - owner * local_states
        for array in (wavefunctions, h_wavefunctions):
            block = lax.dynamic_slice_in_dim(array, offset, BLOCK, 1)
            columns.append(jnp.where(state == owner, block, 0))
    columns = columns[::2] + columns[1::2]
    columns = lax.psum(jnp.concatenate(columns, axis=1), "state")
    full = jnp.dot(
        wavefunctions.T, columns, preferred_element_type=jnp.float32, precision=lax.Precision.HIGH
    )
    mine = lax.psum_scatter(full, "node", scatter_dimension=0, tiled=True)
    return mine[:, : NBLK * BLOCK], mine[:, NBLK * BLOCK :]


def solution(mesh):
    node_count, state_count = mesh.shape["node"], mesh.shape["state"]

    def body(wavefunctions, h_wavefunctions, block_ids):
        share_rows = wavefunctions.shape[1] // node_count
        fits = node_count == 16 and state_count == 2 and share_rows % LANES == 0
        return (halved if fits else gathered)(wavefunctions, h_wavefunctions, block_ids)

    placed = (P("node", "state"), P("node", "state"), P())
    return jax.shard_map(
        body,
        mesh=mesh,
        in_specs=placed,
        out_specs=(P(("state", "node"), None), P(("state", "node"), None)),
        check_vma=False,
    )
```

```python
import functools

import jax
import jax.numpy as jnp
from jax import lax
from jax.experimental import pallas as pl
from jax.experimental.pallas import tpu as pltpu
from jax.sharding import PartitionSpec as P

BLOCK = 128
NBLK = 4
LANES = 128
BUFFERS = 4
STEPS = 8
FLOPS = 115_000_000
VMEM = 32 << 20

BITS = {"x": 1, "y": 2, "z": 4, "w": 8}

GROUPS = (
    (("yzxw", 136), ("xzyw", 120)),
    (("yzxw", 104), ("xyzw", 144), ("xzwy", 136)),
    (("yzxw", 176), ("zyxw", 104), ("xyzw", 104)),
)

ORDER = (
    ("0", 50), ("1", 70), (1, 6), (0, 3), ("2", 52), (1, 3), (2, 13), (0, 3), (3, 5), (1, 18), (0, 3),
    (2, 21), (3, 3), (2, 25), (3, 48), (4, 14), (6, 21), (5, 17), (4, 6), (7, 6), (6, 22), (6, 8), (7, 3),
    (4, 3), (5, 20), (7, 12), (5, 6),
)


def split(value):
    high = value.astype(jnp.bfloat16)
    low = (value - high.astype(jnp.float32)).astype(jnp.bfloat16)
    return high, low


def ranked(info, rank, local_blocks):
    owned = [(lax.div(info[i], local_blocks) == info[NBLK + 1]).astype(jnp.int32) for i in range(NBLK)]
    mine = sum(owned)
    place, slot = 0, 0
    for i in range(NBLK):
        at = jnp.where(owned[i] == 1, sum(owned[:i]), mine + i - sum(owned[:i]))
        place = jnp.where(at == rank, lax.rem(info[i], local_blocks), place)
        slot = jnp.where(at == rank, i, slot)
    return place, slot


def owned_count(info, local_blocks):
    return sum((lax.div(info[i], local_blocks) == info[NBLK + 1]).astype(jnp.int32) for i in range(NBLK))


def bit_of(step, axis):
    shift = {"y": 2, "z": 1, "w": 0}[axis]
    return (step >> shift) & 1


def taken(step, axis, sent):
    bit = {"y": 4, "z": 2, "w": 1}[axis]
    before = step & -(2 * bit)
    if sent:
        return jnp.where(step & bit, step, jnp.maximum(before - 1, bit))
    return jnp.where(step & bit, before + bit - 1, step)


def partial_kernel(info, *refs, outs, first, local_blocks):
    states_ref, refs = refs[0], refs[1:]
    if first == 0:
        source_refs, refs = refs[:1], refs[1:]
    else:
        source_refs, refs = refs[:2], refs[3:]
    out_refs, refs = refs[: len(outs)], refs[len(outs) :]
    if first == 0:
        own_ref, *refs, held_ref, held_sem, own_sem = refs
    columns_ref, stack_ref, block_ref, columns_sem, sem = refs
    blocks = columns_ref.shape[0]
    width = blocks * BLOCK
    share_rows = block_ref.shape[2] // 2
    step = pl.program_id(0)

    def fetch(at):
        copies = []
        for half in range(2):
            relative = (bit_of(at, "y") << 1) | (bit_of(at, "z") << 2) | (bit_of(at, "w") << 3) | half
            group = relative ^ info[NBLK]
            copies.append(
                pltpu.make_async_copy(
                    states_ref.at[:, pl.ds(pl.multiple_of(group * share_rows, share_rows), share_rows)],
                    block_ref.at[at % BUFFERS, :, pl.ds(half * share_rows, share_rows)],
                    sem.at[at % BUFFERS, half],
                )
            )
        return copies

    def gather(rank, which):
        place = ranked(info, rank, local_blocks)[0]
        columns = pl.ds(pl.multiple_of(place * BLOCK, BLOCK), BLOCK)
        source = (states_ref, source_refs[0])[which]
        return pltpu.make_async_copy(source.at[:, columns], held_ref.at[rank, which], held_sem.at[rank, which])

    def hand_over():
        return pltpu.make_async_copy(held_ref, own_ref, own_sem)

    @pl.when(step == 0)
    def _():
        mine = owned_count(info, local_blocks)
        for block in range(blocks):
            rank, which = divmod(first // BLOCK + block, 2)
            here, semaphore = columns_ref.at[block], columns_sem.at[block]

            def bring(source, at):
                pltpu.make_async_copy(source.at[at, which], here, semaphore).start()

            if first == 0:
                gather(rank, which).start()
            else:
                pl.when(rank < mine)(functools.partial(bring, source_refs[0], min(rank, NBLK - 2)))
                pl.when(rank >= mine)(
                    functools.partial(bring, source_refs[1], jnp.clip(rank - mine, 0, NBLK - 2))
                )
        for ahead in range(BUFFERS):
            for copy in fetch(ahead):
                copy.start()
        if first == 0:
            for block in range(blocks, 2 * (NBLK - 1)):
                gather(*divmod(block, 2)).start()
        for block in range(blocks):
            if first == 0:
                gather(*divmod(block, 2)).wait()
                columns = held_ref[block // 2, block % 2]
            else:
                here = columns_ref.at[block]
                pltpu.make_async_copy(here, here, columns_sem.at[block]).wait()
                columns = columns_ref[block]
            rows = pl.ds(block * BLOCK, BLOCK)
            low_rows = pl.ds(width + block * BLOCK, BLOCK)
            stack_ref[rows], stack_ref[low_rows] = split(columns.T)

    @pl.when((step >= 1) & (step + BUFFERS - 1 < STEPS))
    def _():
        for copy in fetch(step + BUFFERS - 1):
            copy.start()

    for copy in fetch(step):
        copy.wait()
    multiply(step, block_ref.at[step % BUFFERS], stack_ref, outs, out_refs)

    if first == 0:

        @pl.when(step == STEPS // 2)
        def _():
            for block in range(blocks, 2 * (NBLK - 1)):
                gather(*divmod(block, 2)).wait()
            hand_over().start()

        @pl.when(step == STEPS - 1)
        def _():
            hand_over().wait()


def multiply(step, block_ref, stack_ref, outs, out_refs):
    width = stack_ref.shape[0] // 2
    share_rows = block_ref.shape[1] // 2
    dot = functools.partial(jnp.dot, preferred_element_type=jnp.float32)
    high, low = split(block_ref[...])
    both = dot(stack_ref[...], high)
    result = both[:width] + (both[width:] + dot(stack_ref[:width], low))
    halves = (result[:, :share_rows], result[:, share_rows:])
    for (bits, start, size, sent), out_ref in zip(outs, out_refs):
        if bits[0] == "x":
            out_ref[0, 0, 0] = halves[sent][start : start + size]
            continue
        at = bits.index("x") - 1

        @pl.when(bit_of(step, bits[0]) == sent)
        def _():
            for half in range(2):
                index = tuple(half if k == at else 0 for k in range(3))
                out_ref[index] = halves[half][start : start + size]


def partial_sums(wavefunctions, sources, info, share_rows, parts, first, beside):
    nodes = wavefunctions.shape[0]
    width = sum(size for _, size in parts)
    outs = []
    for sent in (1, 0):
        start = 0
        for bits, size in parts:
            outs.append((bits, start, size, sent))
            start += size

    def spec(bits, start, size, sent):
        def index(step, info):
            if bits[0] != "x":
                step = taken(step, bits[0], sent)
            return (*(0 if b == "x" else bit_of(step, b) for b in bits[1:]), 0, 0)

        return pl.BlockSpec((*(2 if b == "x" else 1 for b in bits[1:]), size, share_rows), index)

    columns = []
    if first == 0:
        columns = [jax.ShapeDtypeStruct((NBLK - 1, 2, nodes, BLOCK), jnp.float32)]
    made = pl.pallas_call(
        functools.partial(
            partial_kernel,
            outs=outs,
            first=first,
            local_blocks=wavefunctions.shape[1] // BLOCK,
        ),
        grid_spec=pltpu.PrefetchScalarGridSpec(
            num_scalar_prefetch=1,
            grid=(STEPS,),
            in_specs=[pl.BlockSpec(memory_space=pl.ANY)] * (len(sources) + 1),
            out_specs=[spec(*out) for out in outs] + [pl.BlockSpec(memory_space=pl.ANY)] * len(columns),
            scratch_shapes=[
                pltpu.VMEM((width // BLOCK, nodes, BLOCK), jnp.float32),
                pltpu.VMEM((2 * width, nodes), jnp.bfloat16),
                pltpu.VMEM((BUFFERS, nodes, 2 * share_rows), jnp.float32),
                pltpu.SemaphoreType.DMA((width // BLOCK,)),
                pltpu.SemaphoreType.DMA((BUFFERS, 2)),
            ]
            + [
                scratch
                for shape in columns
                for scratch in (
                    pltpu.VMEM(shape.shape, shape.dtype),
                    pltpu.SemaphoreType.DMA((NBLK - 1, 2)),
                    pltpu.SemaphoreType.DMA,
                )
            ],
        ),
        out_shape=[jax.ShapeDtypeStruct((2, 2, 2, out[2], share_rows), jnp.float32) for out in outs] + columns,
        compiler_params=pltpu.CompilerParams(vmem_limit_bytes=VMEM),
        cost_estimate=pl.CostEstimate(
            flops=beside * FLOPS,
            bytes_accessed=8 * STEPS * share_rows * (nodes + width),
            transcendentals=0,
        ),
        name="partial_sums",
    )(info, wavefunctions, *sources)
    return [m.reshape(8, *m.shape[3:]) for m in made[: len(outs)]] + list(made[len(outs) :])


def total(leaves, at):
    value = leaves[0][at]
    for leaf in leaves[1:]:
        value = value + leaf[at]
    return value


def add_kernel(*refs):
    refs[-1][0] = total(refs[:-2], 0)


def add_up(leaves, count, token, beside):
    shape = leaves[0].shape[1:]
    return pl.pallas_call(
        add_kernel,
        grid=(count,),
        in_specs=[pl.BlockSpec((1, *shape), lambda i: (count + i, 0, 0))] * len(leaves)
        + [pl.BlockSpec(memory_space=pl.ANY)],
        out_specs=pl.BlockSpec((1, *shape), lambda i: (i, 0, 0)),
        out_shape=jax.ShapeDtypeStruct((count, *shape), jnp.float32),
        compiler_params=pltpu.CompilerParams(vmem_limit_bytes=16 << 20),
        cost_estimate=pl.CostEstimate(
            flops=beside * FLOPS,
            bytes_accessed=4 * count * shape[0] * shape[1] * (len(leaves) + 1),
            transcendentals=0,
        ),
        name="add_up",
    )(*leaves, token)


def place_kernel(info, sums_ref, correlation_ref, energy_ref):
    correlation_ref[...] = sums_ref[0, :BLOCK, :].T
    energy_ref[...] = sums_ref[0, BLOCK:, :].T


def place_columns(sums, info, share_rows, local_blocks):
    out = jax.ShapeDtypeStruct((share_rows, NBLK * BLOCK), jnp.float32)
    target = pl.BlockSpec((share_rows, BLOCK), lambda i, info: (0, ranked(info, i, local_blocks)[1]))
    return pl.pallas_call(
        place_kernel,
        grid_spec=pltpu.PrefetchScalarGridSpec(
            num_scalar_prefetch=1,
            grid=(NBLK,),
            in_specs=[pl.BlockSpec((1, 2 * BLOCK, share_rows), lambda i, info: (i, 0, 0))],
            out_specs=[target, target],
        ),
        out_shape=[out, out],
        compiler_params=pltpu.CompilerParams(vmem_limit_bytes=24 << 20),
        name="place_columns",
    )(info, sums)


def swap(value, axis):
    bit = BITS[axis]
    return lax.ppermute(value, "node", [(i, i ^ bit) for i in range(lax.axis_size("node"))])


def swap_cores(value):
    return lax.ppermute(value, "state", [(0, 1), (1, 0)])


def other_columns(first, more, other, owned_count):
    own, other = jnp.concatenate([first, more]), jnp.concatenate(other)
    return jnp.concatenate(
        [
            jnp.where(
                i < owned_count,
                own[min(i, NBLK - 2)],
                lax.dynamic_index_in_dim(other, jnp.clip(i - owned_count, 0, NBLK - 2), 0, False),
            )
            for i in range(1, NBLK)
        ]
    )


def halved(wavefunctions, h_wavefunctions, block_ids):
    local_states = wavefunctions.shape[1]
    share_rows = local_states // lax.axis_size("node")
    local_blocks = local_states // BLOCK
    info = jnp.concatenate([block_ids, lax.axis_index("node")[None], lax.axis_index("state")[None]])

    held = {}
    first = 0
    for step, beside in ORDER:
        if isinstance(step, str):
            group = int(step)
            parts = GROUPS[group]
            sources = [own, other, last] if group else [h_wavefunctions]
            out = partial_sums(wavefunctions, sources, info, share_rows, parts, first, beside)
            last = out[0]
            if group == 0:
                own = out.pop()
                other = swap_cores(own)
            first += sum(size for _, size in parts)
            sent, kept = out[: len(parts)], out[len(parts) :]
            for (bits, size), send, keep in zip(parts, sent, kept):
                held[len(held)] = (bits, [keep, swap(send, bits[0])])
        else:
            bits, leaves = held[step]
            turn = len(leaves) - 1
            last = add_up(leaves, 8 >> turn, last, beside)
            leaves.append(swap(last, bits[turn]))
    results = [total(leaves, 0) for _, leaves in held.values()]
    sums = jnp.concatenate(results).reshape(NBLK, 2 * BLOCK, share_rows)
    return tuple(place_columns(sums, info, share_rows, local_blocks))


def gathered(wavefunctions, h_wavefunctions, block_ids):
    local_states = wavefunctions.shape[1]
    state = lax.axis_index("state")
    columns = []
    for step in range(NBLK):
        first = block_ids[step] * BLOCK
        owner = first // local_states
        offset = first - owner * local_states
        for array in (wavefunctions, h_wavefunctions):
            block = lax.dynamic_slice_in_dim(array, offset, BLOCK, 1)
            columns.append(jnp.where(state == owner, block, 0))
    columns = columns[::2] + columns[1::2]
    columns = lax.psum(jnp.concatenate(columns, axis=1), "state")
    full = jnp.dot(
        wavefunctions.T, columns, preferred_element_type=jnp.float32, precision=lax.Precision.HIGH
    )
    mine = lax.psum_scatter(full, "node", scatter_dimension=0, tiled=True)
    return mine[:, : NBLK * BLOCK], mine[:, NBLK * BLOCK :]


def solution(mesh):
    node_count, state_count = mesh.shape["node"], mesh.shape["state"]

    def body(wavefunctions, h_wavefunctions, block_ids):
        share_rows = wavefunctions.shape[1] // node_count
        fits = node_count == 16 and state_count == 2 and share_rows % LANES == 0
        return (halved if fits else gathered)(wavefunctions, h_wavefunctions, block_ids)

    placed = (P("node", "state"), P("node", "state"), P())
    return jax.shard_map(
        body,
        mesh=mesh,
        in_specs=placed,
        out_specs=(P(("state", "node"), None), P(("state", "node"), None)),
        check_vma=False,
    )
```

```python
import functools

import jax
import jax.numpy as jnp
from jax import lax
from jax.experimental import pallas as pl
from jax.experimental.pallas import tpu as pltpu
from jax.sharding import PartitionSpec as P

BLOCK = 128
NBLK = 4
LANES = 128
BUFFERS = 4
STEPS = 8
FLOPS = 115_000_000
VMEM = 32 << 20

BITS = {"x": 1, "y": 2, "z": 4, "w": 8}

GROUPS = (
    (("yzxw", 136), ("xzyw", 120)),
    (("yzxw", 112), ("xyzw", 152), ("xzwy", 120)),
    (("yzxw", 144), ("zyxw", 104), ("xyzw", 136)),
)

ORDER = (
    ("0", 80), ("1", 70), ((1,), 6), ((0,), 3), ("2", 52), ((1,), 3), ((2,), 13), ((3,), 5), ((0,), 3),
    ((1,), 18), ((0,), 0), ((2,), 21), ((3,), 0), ((2,), 25), ((3,), 48), ((4,), 14), ((6,), 20), ((5,), 17),
    ((4,), 20), ((7,), 6), ((6,), 22), ((7,), 3), ((4,), 1), ((5,), 6), ((6,), 8), ((5,), 40), ((7,), 18),
)


def split(value):
    high = value.astype(jnp.bfloat16)
    low = (value - high.astype(jnp.float32)).astype(jnp.bfloat16)
    return high, low


def ranked(info, rank, local_blocks):
    owned = [(lax.div(info[i], local_blocks) == info[NBLK + 1]).astype(jnp.int32) for i in range(NBLK)]
    mine = sum(owned)
    place, slot = 0, 0
    for i in range(NBLK):
        at = jnp.where(owned[i] == 1, sum(owned[:i]), mine + i - sum(owned[:i]))
        place = jnp.where(at == rank, lax.rem(info[i], local_blocks), place)
        slot = jnp.where(at == rank, i, slot)
    return place, slot


def owned_count(info, local_blocks):
    return sum((lax.div(info[i], local_blocks) == info[NBLK + 1]).astype(jnp.int32) for i in range(NBLK))


def bit_of(step, axis):
    shift = {"y": 2, "z": 1, "w": 0}[axis]
    return (step >> shift) & 1


def taken(step, axis, sent):
    bit = {"y": 4, "z": 2, "w": 1}[axis]
    before = step & -(2 * bit)
    if sent:
        return jnp.where(step & bit, step, jnp.maximum(before - 1, bit))
    return jnp.where(step & bit, before + bit - 1, step)


def partial_kernel(info, *refs, outs, first, local_blocks):
    states_ref, refs = refs[0], refs[1:]
    if first == 0:
        source_refs, refs = refs[:1], refs[1:]
    else:
        source_refs, refs = refs[:2], refs[3:]
    out_refs, refs = refs[: len(outs)], refs[len(outs) :]
    if first == 0:
        own_ref, *refs, held_ref, held_sem, own_sem = refs
    columns_ref, stack_ref, block_ref, columns_sem, sem = refs
    blocks = columns_ref.shape[0]
    width = blocks * BLOCK
    share_rows = block_ref.shape[2] // 2
    step = pl.program_id(0)

    def fetch(at):
        copies = []
        for half in range(2):
            relative = (bit_of(at, "y") << 1) | (bit_of(at, "z") << 2) | (bit_of(at, "w") << 3) | half
            group = relative ^ info[NBLK]
            copies.append(
                pltpu.make_async_copy(
                    states_ref.at[:, pl.ds(pl.multiple_of(group * share_rows, share_rows), share_rows)],
                    block_ref.at[at % BUFFERS, :, pl.ds(half * share_rows, share_rows)],
                    sem.at[at % BUFFERS, half],
                )
            )
        return copies

    def gather(rank, which):
        place = ranked(info, rank, local_blocks)[0]
        columns = pl.ds(pl.multiple_of(place * BLOCK, BLOCK), BLOCK)
        source = (states_ref, source_refs[0])[which]
        return pltpu.make_async_copy(source.at[:, columns], held_ref.at[rank, which], held_sem.at[rank, which])

    def hand_over():
        return pltpu.make_async_copy(held_ref, own_ref, own_sem)

    @pl.when(step == 0)
    def _():
        mine = owned_count(info, local_blocks)
        for block in range(blocks):
            rank, which = divmod(first // BLOCK + block, 2)
            here, semaphore = columns_ref.at[block], columns_sem.at[block]

            def bring(source, at):
                pltpu.make_async_copy(source.at[at, which], here, semaphore).start()

            if first == 0:
                gather(rank, which).start()
            else:
                pl.when(rank < mine)(functools.partial(bring, source_refs[0], min(rank, NBLK - 2)))
                pl.when(rank >= mine)(
                    functools.partial(bring, source_refs[1], jnp.clip(rank - mine, 0, NBLK - 2))
                )
        for ahead in range(BUFFERS):
            for copy in fetch(ahead):
                copy.start()
        if first == 0:
            for block in range(blocks, 2 * (NBLK - 1)):
                gather(*divmod(block, 2)).start()
        for block in range(blocks):
            if first == 0:
                gather(*divmod(block, 2)).wait()
                columns = held_ref[block // 2, block % 2]
            else:
                here = columns_ref.at[block]
                pltpu.make_async_copy(here, here, columns_sem.at[block]).wait()
                columns = columns_ref[block]
            rows = pl.ds(block * BLOCK, BLOCK)
            low_rows = pl.ds(width + block * BLOCK, BLOCK)
            stack_ref[rows], stack_ref[low_rows] = split(columns.T)

    @pl.when((step >= 1) & (step + BUFFERS - 1 < STEPS))
    def _():
        for copy in fetch(step + BUFFERS - 1):
            copy.start()

    for copy in fetch(step):
        copy.wait()
    multiply(step, block_ref.at[step % BUFFERS], stack_ref, outs, out_refs)

    if first == 0:

        @pl.when(step == STEPS // 2)
        def _():
            for block in range(blocks, 2 * (NBLK - 1)):
                gather(*divmod(block, 2)).wait()
            hand_over().start()

        @pl.when(step == STEPS - 1)
        def _():
            hand_over().wait()


def multiply(step, block_ref, stack_ref, outs, out_refs):
    width = stack_ref.shape[0] // 2
    share_rows = block_ref.shape[1] // 2
    dot = functools.partial(jnp.dot, preferred_element_type=jnp.float32)
    high, low = split(block_ref[...])
    both = dot(stack_ref[...], high)
    result = both[:width] + (both[width:] + dot(stack_ref[:width], low))
    halves = (result[:, :share_rows], result[:, share_rows:])
    for (bits, start, size, sent), out_ref in zip(outs, out_refs):
        if bits[0] == "x":
            out_ref[0, 0, 0] = halves[sent][start : start + size]
            continue
        at = bits.index("x") - 1

        @pl.when(bit_of(step, bits[0]) == sent)
        def _():
            for half in range(2):
                index = tuple(half if k == at else 0 for k in range(3))
                out_ref[index] = halves[half][start : start + size]


def partial_sums(wavefunctions, sources, info, share_rows, parts, first, beside):
    nodes = wavefunctions.shape[0]
    width = sum(size for _, size in parts)
    outs = []
    for sent in (1, 0):
        start = 0
        for bits, size in parts:
            outs.append((bits, start, size, sent))
            start += size

    def spec(bits, start, size, sent):
        def index(step, info):
            if bits[0] != "x":
                step = taken(step, bits[0], sent)
            return (*(0 if b == "x" else bit_of(step, b) for b in bits[1:]), 0, 0)

        return pl.BlockSpec((*(2 if b == "x" else 1 for b in bits[1:]), size, share_rows), index)

    columns = []
    if first == 0:
        columns = [jax.ShapeDtypeStruct((NBLK - 1, 2, nodes, BLOCK), jnp.float32)]
    made = pl.pallas_call(
        functools.partial(
            partial_kernel,
            outs=outs,
            first=first,
            local_blocks=wavefunctions.shape[1] // BLOCK,
        ),
        grid_spec=pltpu.PrefetchScalarGridSpec(
            num_scalar_prefetch=1,
            grid=(STEPS,),
            in_specs=[pl.BlockSpec(memory_space=pl.ANY)] * (len(sources) + 1),
            out_specs=[spec(*out) for out in outs] + [pl.BlockSpec(memory_space=pl.ANY)] * len(columns),
            scratch_shapes=[
                pltpu.VMEM((width // BLOCK, nodes, BLOCK), jnp.float32),
                pltpu.VMEM((2 * width, nodes), jnp.bfloat16),
                pltpu.VMEM((BUFFERS, nodes, 2 * share_rows), jnp.float32),
                pltpu.SemaphoreType.DMA((width // BLOCK,)),
                pltpu.SemaphoreType.DMA((BUFFERS, 2)),
            ]
            + [
                scratch
                for shape in columns
                for scratch in (
                    pltpu.VMEM(shape.shape, shape.dtype),
                    pltpu.SemaphoreType.DMA((NBLK - 1, 2)),
                    pltpu.SemaphoreType.DMA,
                )
            ],
        ),
        out_shape=[jax.ShapeDtypeStruct((2, 2, 2, out[2], share_rows), jnp.float32) for out in outs] + columns,
        compiler_params=pltpu.CompilerParams(vmem_limit_bytes=VMEM),
        cost_estimate=pl.CostEstimate(
            flops=beside * FLOPS,
            bytes_accessed=8 * STEPS * share_rows * (nodes + width),
            transcendentals=0,
        ),
        name="partial_sums",
    )(info, wavefunctions, *sources)
    return [m.reshape(8, *m.shape[3:]) for m in made[: len(outs)]] + list(made[len(outs) :])


def add_kernel(*refs, parts):
    refs, out_ref = refs[:-2], refs[-1]
    start = 0
    for width, leaves in parts:
        value = None
        for number, row in leaves:
            term = refs[number][0, row : row + width]
            value = term if value is None else value + term
        out_ref[0, start : start + width] = value
        start += width


def add_up(stream, count, token, beside):
    arrays = []
    parts = []
    for width, leaves in stream:
        numbers = []
        for array, row in leaves:
            if not any(array is other for other in arrays):
                arrays.append(array)
            numbers.append(([array is other for other in arrays].index(True), row))
        parts.append((width, numbers))
    width = sum(part[0] for part in parts)
    share_rows = arrays[0].shape[2]
    size = sum(array.shape[1] for array in arrays) + width
    return pl.pallas_call(
        functools.partial(add_kernel, parts=parts),
        grid=(count,),
        in_specs=[pl.BlockSpec((1, *array.shape[1:]), lambda i: (count + i, 0, 0)) for array in arrays]
        + [pl.BlockSpec(memory_space=pl.ANY)],
        out_specs=pl.BlockSpec((1, width, share_rows), lambda i: (i, 0, 0)),
        out_shape=jax.ShapeDtypeStruct((count, width, share_rows), jnp.float32),
        compiler_params=pltpu.CompilerParams(vmem_limit_bytes=16 << 20),
        cost_estimate=pl.CostEstimate(
            flops=beside * FLOPS, bytes_accessed=4 * count * share_rows * size, transcendentals=0
        ),
        name="add_up",
    )(*arrays, token)


def place_kernel(info, sums_ref, correlation_ref, energy_ref):
    correlation_ref[...] = sums_ref[0, :BLOCK, :].T
    energy_ref[...] = sums_ref[0, BLOCK:, :].T


def place_columns(sums, info, share_rows, local_blocks):
    out = jax.ShapeDtypeStruct((share_rows, NBLK * BLOCK), jnp.float32)
    target = pl.BlockSpec((share_rows, BLOCK), lambda i, info: (0, ranked(info, i, local_blocks)[1]))
    return pl.pallas_call(
        place_kernel,
        grid_spec=pltpu.PrefetchScalarGridSpec(
            num_scalar_prefetch=1,
            grid=(NBLK,),
            in_specs=[pl.BlockSpec((1, 2 * BLOCK, share_rows), lambda i, info: (i, 0, 0))],
            out_specs=[target, target],
        ),
        out_shape=[out, out],
        compiler_params=pltpu.CompilerParams(vmem_limit_bytes=24 << 20),
        name="place_columns",
    )(info, sums)


def swap(value, axis):
    bit = BITS[axis]
    return lax.ppermute(value, "node", [(i, i ^ bit) for i in range(lax.axis_size("node"))])


def swap_cores(value):
    return lax.ppermute(value, "state", [(0, 1), (1, 0)])


def other_columns(first, more, other, owned_count):
    own, other = jnp.concatenate([first, more]), jnp.concatenate(other)
    return jnp.concatenate(
        [
            jnp.where(
                i < owned_count,
                own[min(i, NBLK - 2)],
                lax.dynamic_index_in_dim(other, jnp.clip(i - owned_count, 0, NBLK - 2), 0, False),
            )
            for i in range(1, NBLK)
        ]
    )


def halved(wavefunctions, h_wavefunctions, block_ids):
    local_states = wavefunctions.shape[1]
    share_rows = local_states // lax.axis_size("node")
    local_blocks = local_states // BLOCK
    info = jnp.concatenate([block_ids, lax.axis_index("node")[None], lax.axis_index("state")[None]])

    streams, parts_made = {}, []
    first = 0
    for step, beside in ORDER:
        if isinstance(step, str):
            group = int(step)
            parts = GROUPS[group]
            sources = [own, other, last] if group else [h_wavefunctions]
            out = partial_sums(wavefunctions, sources, info, share_rows, parts, first, beside)
            last = out[0]
            if group == 0:
                own = out.pop()
                other = swap_cores(own)
            first += sum(size for _, size in parts)
            for (bits, size), send, keep in zip(parts, out[: len(parts)], out[len(parts) :]):
                part = (size, [(keep, 0), (swap(send, bits[0]), 0)])
                streams[len(parts_made)] = (bits[1:], [part])
                parts_made.append(part)
        else:
            bits = streams[step[0]][0]
            stream = [part for number in step for part in streams[number][1]]
            last = add_up(stream, 1 << (len(bits) - 1), last, beside)
            received = swap(last, bits[0])
            row = 0
            for size, leaves in stream:
                leaves.append((received, row))
                row += size
            streams[step[0]] = (bits[1:], stream)
    results = []
    for size, leaves in parts_made:
        terms = [array[0, row : row + size] for array, row in leaves]
        results.append(sum(terms[1:], terms[0]))
    sums = jnp.concatenate(results).reshape(NBLK, 2 * BLOCK, share_rows)
    return tuple(place_columns(sums, info, share_rows, local_blocks))


def gathered(wavefunctions, h_wavefunctions, block_ids):
    local_states = wavefunctions.shape[1]
    state = lax.axis_index("state")
    columns = []
    for step in range(NBLK):
        first = block_ids[step] * BLOCK
        owner = first // local_states
        offset = first - owner * local_states
        for array in (wavefunctions, h_wavefunctions):
            block = lax.dynamic_slice_in_dim(array, offset, BLOCK, 1)
            columns.append(jnp.where(state == owner, block, 0))
    columns = columns[::2] + columns[1::2]
    columns = lax.psum(jnp.concatenate(columns, axis=1), "state")
    full = jnp.dot(
        wavefunctions.T, columns, preferred_element_type=jnp.float32, precision=lax.Precision.HIGH
    )
    mine = lax.psum_scatter(full, "node", scatter_dimension=0, tiled=True)
    return mine[:, : NBLK * BLOCK], mine[:, NBLK * BLOCK :]


def solution(mesh):
    node_count, state_count = mesh.shape["node"], mesh.shape["state"]

    def body(wavefunctions, h_wavefunctions, block_ids):
        share_rows = wavefunctions.shape[1] // node_count
        fits = node_count == 16 and state_count == 2 and share_rows % LANES == 0
        return (halved if fits else gathered)(wavefunctions, h_wavefunctions, block_ids)

    placed = (P("node", "state"), P("node", "state"), P())
    return jax.shard_map(
        body,
        mesh=mesh,
        in_specs=placed,
        out_specs=(P(("state", "node"), None), P(("state", "node"), None)),
        check_vma=False,
    )
```
